32 devices in a mesh: dp: 8 (over z, core), land: 4 (over y, x).
Axes of the slice: x: 2, y: 2, z: 4, core: 2. Of those that a mesh axis runs over, the one named last changes fastest.
Arguments:
- doc_values: bfloat16 [12288, 1024], P('dp'), may hold values from 0 to 100
- doc_blocks: int32 [96, 8], P('dp'), may hold values from 0 to 511, as said below
- land_values: bfloat16 [16384, 1024], P(('dp', 'land')), may hold values from 0 to 100
- land_blocks: int32 [128, 8], replicated, may hold values from 0 to 511, as said below
- coefficients: bfloat16 [16384, 64], P(('dp', 'land')), may hold values from -12 to 12
Outputs:
- normal_product: float32 [16384, 64], P(('dp', 'land'))
The draws below stay inside these ranges and needn't reach their ends.
Inputs may be any that keep to these rules, and one draw needn't show every extreme that they name: `doc_blocks`: each row lists 8 different vocabulary block numbers. `land_blocks`: each row lists 8 different vocabulary block numbers.
All inputs are finite; a program needn't handle non-finite values.
Results may differ from the reference program's by a relative error of at most 0.0003.
Values may be sent and summed in bfloat16 or wider, within the bound.
A program may use at most 128 MiB of HBM per device.

```python
import math
import jax
import jax.numpy as jnp
from jax import lax

VOCAB_BLOCKS = 512
TERM_BLOCK = 128
ACTIVE = 8
LAND_ACTIVE = 8
DOC_BLOCK = 128
LM_BLOCK = 128
TARGETS = 64
LANDMARKS = 16384
DOCS = 12288


topic_count = 4


def block_lists(key, salt, rows, picks):
    popular = jax.random.permutation(jax.random.fold_in(key, 11), VOCAB_BLOCKS).astype(jnp.int32)
    numbers = jnp.arange(VOCAB_BLOCKS, dtype=jnp.int32)
    common = (numbers == 0) | (numbers == VOCAB_BLOCKS - 1)
    popular = jnp.where(common, VOCAB_BLOCKS + 64, popular).astype(jnp.int32)
    noise = jax.random.randint(jax.random.fold_in(key, salt), (rows, VOCAB_BLOCKS), 0, 1024)
    scores = (popular[None, :] * 32 + noise) * VOCAB_BLOCKS + numbers[None, :]
    _, chosen = jax.lax.top_k(scores, picks)
    return chosen.astype(jnp.int32)


def block_profiles(key):
    base = jax.random.fold_in(key, 41)
    shape = (VOCAB_BLOCKS, TERM_BLOCK)
    owner = jax.random.randint(jax.random.fold_in(base, 1), shape, 0, topic_count).astype(jnp.int32)
    present = jax.random.uniform(jax.random.fold_in(base, 2), shape) < 0.6
    levels = jnp.exp(jax.random.uniform(jax.random.fold_in(base, 3), shape, minval=math.log(0.1), maxval=0.0))
    idf = jnp.exp(jax.random.uniform(jax.random.fold_in(base, 4), shape, minval=0.0, maxval=math.log(10.0)))
    numbers = jnp.arange(VOCAB_BLOCKS, dtype=jnp.int32)
    common = (numbers == 0) | (numbers == VOCAB_BLOCKS - 1)
    block_scale = jnp.where(common, 3.0, 1.0).astype(jnp.float32)
    weight = idf * block_scale[:, None]
    profile = jnp.where(present, levels, 0.0) * weight
    return (owner, profile.astype(jnp.float32), weight.astype(jnp.float32))


def term_values(key, salt, lists, row_block):
    block_total = lists.shape[0]
    picks = lists.shape[1]
    width = picks * TERM_BLOCK
    rows = block_total * row_block
    owner, profile, weight = block_profiles(key)
    owner_rows = owner[lists].reshape(block_total, 1, width)
    profile_rows = profile[lists].reshape(block_total, 1, width)
    weight_rows = weight[lists].reshape(block_total, 1, width)
    base = jax.random.fold_in(key, salt)
    exponent = 2.5 * jax.random.normal(jax.random.fold_in(base, 5), (block_total, row_block, topic_count))
    mixing = jnp.exp(exponent - jnp.max(exponent, axis=2, keepdims=True))
    selected = jnp.zeros((block_total, row_block, width), jnp.float32)
    for topic in range(topic_count):
        selected = selected + jnp.where(owner_rows == topic, mixing[:, :, topic:topic + 1], 0.0)
    speckle = jax.random.uniform(jax.random.fold_in(base, 6), (block_total, row_block, width)) < 0.3
    amount = jax.random.uniform(jax.random.fold_in(base, 7), (block_total, row_block, width), minval=0.0, maxval=0.4)
    noise = jnp.where(speckle, amount, 0.0) * weight_rows
    values = selected * profile_rows + noise
    values = jnp.minimum(values, 100.0).astype(jnp.float32)
    return values.reshape(rows, width).astype(jnp.bfloat16)


def draw_doc_blocks(key, part):
    return block_lists(key, 13, DOCS // DOC_BLOCK, ACTIVE)


def draw_land_blocks(key, part):
    return block_lists(key, 17, LANDMARKS // LM_BLOCK, LAND_ACTIVE)


def draw_doc_values(key, part):
    lists = block_lists(key, 13, DOCS // DOC_BLOCK, ACTIVE)
    return term_values(key, 101, lists, DOC_BLOCK)


def draw_land_values(key, part):
    lists = block_lists(key, 17, LANDMARKS // LM_BLOCK, LAND_ACTIVE)
    return term_values(key, 202, lists, LM_BLOCK)


def steps_of(own_key, extent, pieces, low, top_value):
    gain = 1.0
    for position, parts in pieces:
        steps = jax.random.uniform(jax.random.fold_in(jax.random.fold_in(own_key, 6), position), (parts,), jnp.float32, low / len(pieces), top_value / len(pieces))
        gain = gain * jnp.repeat(jnp.exp(steps), extent[position] // parts).reshape((-1,) + (1,) * (len(extent) - 1 - position))
    return gain


def centred(own_key, dims, scale, most, pieces=(), held_as=jnp.bfloat16):
    loudness = steps_of(own_key, dims, pieces, -0.22, 0.18) if pieces else 1.0
    values = jax.random.normal(own_key, dims, jnp.float32) * scale * loudness
    return jnp.minimum(jnp.maximum(values, -most), most).astype(held_as)


def setup_inputs(seed: int = 0) -> dict:
    streams_of = jax.random.split(jax.random.key(seed), 6)
    return {
        "doc_values": draw_doc_values(jax.random.fold_in(streams_of[5], 71), 0),
        "doc_blocks": draw_doc_blocks(jax.random.fold_in(streams_of[5], 71), 0),
        "land_values": draw_land_values(jax.random.fold_in(streams_of[5], 71), 0),
        "land_blocks": draw_land_blocks(jax.random.fold_in(streams_of[5], 71), 0),
        "coefficients": centred(streams_of[4], (LANDMARKS, TARGETS), 2.0, 12.0, ((0, 32),)),
    }


sharpness = 2.0

def kernel_block(doc_grid, doc_blocks, doc_norm, tile_grid, tile_ids, tile_norms):
    matches = (doc_blocks[:, :, None] == tile_ids[None, None, :]).astype(jnp.float32)
    aligned = jnp.einsum('dab,lbt->dlat', matches, tile_grid.astype(jnp.float32)).astype(jnp.bfloat16)
    aligned = aligned.reshape(matches.shape[0], LM_BLOCK, ACTIVE * TERM_BLOCK)
    inner_terms = jnp.einsum('drw,dlw->drl', doc_grid.astype(jnp.float32), aligned.astype(jnp.float32))
    inner_terms = inner_terms.reshape(-1, LM_BLOCK)
    cosine = inner_terms * doc_norm[:, None] * tile_norms[None, :]
    kernel = jnp.exp(2.0 * sharpness * (cosine - 1.0))
    high = lax.optimization_barrier(kernel.astype(jnp.bfloat16))
    low = (kernel - high.astype(jnp.float32)).astype(jnp.bfloat16)
    return (high, low)

def reference(doc_values, doc_blocks, land_values, land_blocks, coefficients):
    doc_norm = lax.rsqrt(lax.optimization_barrier(jnp.sum(jnp.square(doc_values.astype(jnp.float32)), axis=1)) + 1e-06)
    land_norm = lax.rsqrt(lax.optimization_barrier(jnp.sum(jnp.square(land_values.astype(jnp.float32)), axis=1)) + 1e-06)
    doc_count = doc_values.shape[0] // DOC_BLOCK
    doc_grid = doc_values.reshape(doc_count, DOC_BLOCK, ACTIVE * TERM_BLOCK)
    land_count = LANDMARKS // LM_BLOCK
    land_grid = land_values.reshape(land_count, LM_BLOCK, LAND_ACTIVE, TERM_BLOCK)
    norm_grid = land_norm.reshape(land_count, LM_BLOCK)
    coef = coefficients.reshape(land_count, LM_BLOCK, TARGETS)

    def fit_block(running, packed):
        tile_grid, tile_ids, tile_norms, block_coef = packed
        high, low = kernel_block(doc_grid, doc_blocks, doc_norm, tile_grid, tile_ids, tile_norms)
        running = running + jnp.dot(high, block_coef, preferred_element_type=jnp.float32)
        running = running + jnp.dot(low, block_coef, preferred_element_type=jnp.float32)
        return (running, None)
    fitted, _ = lax.scan(fit_block, jnp.zeros((DOCS, TARGETS), jnp.float32), (land_grid, land_blocks, norm_grid, coef))
    fitted_high = lax.optimization_barrier(fitted.astype(jnp.bfloat16))
    fitted_low = (fitted - fitted_high.astype(jnp.float32)).astype(jnp.bfloat16)
    fitted_pair = jnp.concatenate([fitted_high, fitted_low], axis=1)

    def back_block(packed):
        tile_grid, tile_ids, tile_norms = packed
        high, low = kernel_block(doc_grid, doc_blocks, doc_norm, tile_grid, tile_ids, tile_norms)
        summed = jnp.dot(high.T, fitted_pair, preferred_element_type=jnp.float32)
        summed = summed + jnp.dot(low.T, fitted_pair, preferred_element_type=jnp.float32)
        return (summed[:, :TARGETS] + summed[:, TARGETS:]) / DOCS
    result = lax.map(back_block, (land_grid, land_blocks, norm_grid))
    return result.reshape(LANDMARKS, TARGETS)
```

```python
import functools
import jax
import jax.numpy as jnp
from jax import lax
from jax.experimental import pallas as pl
from jax.experimental.pallas import tpu as pltpu
from jax.sharding import PartitionSpec as P

TERM_BLOCK = 128
ACTIVE = 8
LAND_ACTIVE = 8
DOC_BLOCK = 128
LM_BLOCK = 128
SHARPNESS = 2.0
LOG2E = 1.4426950408889634
EPS = 1e-06
MESH = pl.DeviceIdType.MESH


def row_squares(rows):
    wide = rows.astype(jnp.float32)
    return jnp.sum(wide * wide, axis=1, keepdims=True)


def fused_kernel(
    dp_count, land_count, total_docs,
    pos_ref, doc_ref, land_ref, coef_ref, out_ref,
    lbuf, cbuf, work, kh, kl, dnorm, fit, fpart, full, fpair, sbuf, pbuf, rbuf,
    local_sem, own_send, own_csend, fz_send, fp_send, cfz_send, cfp_send, lrecv, crecv,
    f1_send, f1_recv, f2_send, f2_recv, p_send, p_recv, r_send, r_recv,
):
    nz = dp_count // 2
    nb = land_ref.shape[0]
    nd = doc_ref.shape[0]
    docs = nd * DOC_BLOCK
    targets = coef_ref.shape[0]
    part_rows = targets // land_count
    me = lax.axis_index("dp")
    ml = lax.axis_index("land")
    z = me // 2
    core = me % 2
    mate = z * 2 + (1 - core)

    barrier = pltpu.get_barrier_semaphore()
    pl.semaphore_signal(barrier, inc=1, device_id=(mate, ml), device_id_type=MESH)
    for off in range(1, nz):
        other = lax.rem(z + off, nz) * 2 + core
        pl.semaphore_signal(barrier, inc=1, device_id=(other, ml), device_id_type=MESH)
    for off in range(1, land_count):
        other = lax.rem(ml + off, land_count)
        pl.semaphore_signal(barrier, inc=1, device_id=(me, other), device_id_type=MESH)
    pl.semaphore_wait(barrier, 1 + (nz - 1) + (land_count - 1))

    def own_copy(b, way, device):
        return pltpu.make_async_remote_copy(
            src_ref=land_ref.at[b], dst_ref=lbuf.at[me, b],
            send_sem=own_send.at[way, b], recv_sem=lrecv.at[me, b],
            device_id=(device, ml), device_id_type=MESH)

    def own_coef(way, device):
        return pltpu.make_async_remote_copy(
            src_ref=coef_ref, dst_ref=cbuf.at[me],
            send_sem=own_csend.at[way], recv_sem=crecv.at[me],
            device_id=(device, ml), device_id_type=MESH)

    def forward(slot, b, send, device):
        return pltpu.make_async_remote_copy(
            src_ref=lbuf.at[slot, b], dst_ref=lbuf.at[slot, b],
            send_sem=send, recv_sem=lrecv.at[slot, b],
            device_id=(device, ml), device_id_type=MESH)

    def forward_coef(slot, send, device):
        return pltpu.make_async_remote_copy(
            src_ref=cbuf.at[slot], dst_ref=cbuf.at[slot],
            send_sem=send, recv_sem=crecv.at[slot],
            device_id=(device, ml), device_id_type=MESH)

    ways = ((0, z > 0, me - 2), (1, z < nz - 1, me + 2))

    def start_own(b, carry):
        for way, there, device in ways:
            @pl.when(there)
            def _():
                @pl.when(b == 0)
                def _():
                    own_coef(way, device).start()
                own_copy(b, way, device).start()

        @pl.when(b == 0)
        def _():
            own_coef(2, mate).start()
        own_copy(b, 2, mate).start()
        return carry

    lax.fori_loop(0, nb, start_own, 0)
    keep_land = pltpu.make_async_copy(land_ref, lbuf.at[me], local_sem.at[0])
    keep_coef = pltpu.make_async_copy(coef_ref, cbuf.at[me], local_sem.at[1])
    keep_land.start()
    keep_coef.start()

    work[LAND_ACTIVE] = jnp.zeros((2 * LM_BLOCK, TERM_BLOCK), jnp.bfloat16)
    fit[...] = jnp.zeros_like(fit)

    def doc_norms(d, carry):
        scale = (2.0 * SHARPNESS * LOG2E) * lax.rsqrt(row_squares(doc_ref[d]) + EPS)
        dnorm[d] = jnp.transpose(jnp.broadcast_to(scale, (DOC_BLOCK, DOC_BLOCK)))[0:8, :]
        return carry

    lax.fori_loop(0, nd, doc_norms, 0)
    keep_land.wait()
    keep_coef.wait()

    def compute(q, b):
        norms = []
        for c in range(2):
            for a in range(LAND_ACTIVE):
                work[a, c * LM_BLOCK:(c + 1) * LM_BLOCK, :] = (
                    lbuf[q * 2 + c, b, :, a * TERM_BLOCK:(a + 1) * TERM_BLOCK])
            norms.append(lax.rsqrt(row_squares(lbuf[q * 2 + c, b]) + EPS))
        norm = jnp.concatenate(norms, axis=0)
        start = pl.multiple_of(b * LM_BLOCK, LM_BLOCK)
        coef = jnp.concatenate(
            [cbuf[q * 2, :, pl.ds(start, LM_BLOCK)], cbuf[q * 2 + 1, :, pl.ds(start, LM_BLOCK)]],
            axis=1)
        unit = q * nb + b

        def doc_pair(i, carry):
            highs, lows = [], []
            for h in range(2):
                d = i * 2 + h
                sides = []
                for c in range(2):
                    first = (((q * 2 + c) * nb + b) * nd + d) * ACTIVE
                    sides.append(jnp.concatenate(
                        [work[pos_ref[first + a], c * LM_BLOCK:(c + 1) * LM_BLOCK, :]
                         for a in range(ACTIVE)], axis=1))
                aligned = jnp.concatenate(sides, axis=0)
                inner = lax.dot_general(
                    aligned, doc_ref[d], (((1,), (1,)), ((), ())),
                    preferred_element_type=jnp.float32)
                power = inner * norm * dnorm[d][0:1, :] - (2.0 * SHARPNESS * LOG2E)
                kernel = jnp.exp2(power)
                high = kernel.astype(jnp.bfloat16)
                highs.append(high)
                lows.append((kernel - high.astype(jnp.float32)).astype(jnp.bfloat16))
            high = jnp.concatenate(highs, axis=1)
            low = jnp.concatenate(lows, axis=1)
            cols = pl.ds(pl.multiple_of(i * 2 * DOC_BLOCK, 2 * DOC_BLOCK), 2 * DOC_BLOCK)
            kh[unit, :, cols] = high
            kl[unit, :, cols] = low
            fit[:, cols] += (
                jnp.dot(coef, high, preferred_element_type=jnp.float32)
                + jnp.dot(coef, low, preferred_element_type=jnp.float32))
            return carry

        lax.fori_loop(0, nd // 2, doc_pair, 0)

    def place(r, way):
        hops = r // nb
        q = z + hops * (2 * way - 1)
        return q, r % nb, (q >= 0) & (q < nz)

    def rounds(r, carry):
        for way, there, device in ways:
            @pl.when(r >= nb)
            def _():
                q, b, valid = place(r, way)
                onward = z + (1 - 2 * way)

                @pl.when(valid)
                def _():
                    slot = q * 2 + core
                    forward(slot, b, fp_send.at[q, b], mate).wait_recv()
                    @pl.when((onward >= 0) & (onward < nz))
                    def _():
                        forward(slot, b, fz_send.at[q, b], onward * 2 + core).start()
                    forward(slot, b, fp_send.at[q, b], mate).start()
                    @pl.when(b == 0)
                    def _():
                        forward_coef(slot, cfp_send.at[q], mate).wait_recv()
                        @pl.when((onward >= 0) & (onward < nz))
                        def _():
                            forward_coef(slot, cfz_send.at[q], onward * 2 + core).start()
                        forward_coef(slot, cfp_send.at[q], mate).start()

        def one_way(way, inner_carry):
            q, b, valid = place(r, way)

            @pl.when(valid & ((r >= nb) | (way == 0)))
            def _():
                slot = q * 2 + 1 - core
                forward(slot, b, fp_send.at[q, b], mate).wait_recv()
                @pl.when(b == 0)
                def _():
                    forward_coef(slot, cfp_send.at[q], mate).wait_recv()
                compute(q, b)
            return inner_carry

        lax.fori_loop(0, 2, one_way, 0)
        return carry

    lax.fori_loop(0, nz * nb, rounds, 0)

    def fit_out(off):
        peer = lax.rem(ml + off, land_count)
        rows = pl.ds(pl.multiple_of(peer * part_rows, part_rows), part_rows)
        return pltpu.make_async_remote_copy(
            src_ref=fit.at[rows], dst_ref=fpart.at[ml],
            send_sem=f1_send.at[off], recv_sem=f1_recv.at[ml],
            device_id=(me, peer), device_id_type=MESH)

    def fit_in(off):
        peer = lax.rem(ml + off, land_count)
        rows = pl.ds(pl.multiple_of(ml * part_rows, part_rows), part_rows)
        return pltpu.make_async_remote_copy(
            src_ref=fit.at[rows], dst_ref=fpart.at[peer],
            send_sem=f1_send.at[off], recv_sem=f1_recv.at[peer],
            device_id=(me, peer), device_id_type=MESH)

    def full_copy(owner, off, sem_slot):
        peer = lax.rem(ml + off, land_count)
        rows = pl.ds(pl.multiple_of(owner * part_rows, part_rows), part_rows)
        return pltpu.make_async_remote_copy(
            src_ref=full.at[rows], dst_ref=full.at[rows],
            send_sem=f2_send.at[off], recv_sem=f2_recv.at[sem_slot],
            device_id=(me, peer), device_id_type=MESH)

    for off in range(1, land_count):
        fit_out(off).start()
    mine = pl.ds(pl.multiple_of(ml * part_rows, part_rows), part_rows)
    total = fit[mine, :]
    for off in range(1, land_count):
        fit_in(off).wait_recv()
        total = total + fpart[lax.rem(ml + off, land_count)]
    full[mine, :] = total
    for off in range(1, land_count):
        full_copy(ml, off, ml).start()
    for off in range(1, land_count):
        peer = lax.rem(ml + off, land_count)
        full_copy(peer, off, peer).wait_recv()
    fitted = full[...]
    fitted_high = fitted.astype(jnp.bfloat16)
    fpair[0:targets, :] = fitted_high
    fpair[targets:, :] = (fitted - fitted_high.astype(jnp.float32)).astype(jnp.bfloat16)

    half = LM_BLOCK // 2
    lane = lax.broadcasted_iota(jnp.int32, (half, 2 * targets), 1)

    def mate_copy(q):
        return pltpu.make_async_remote_copy(
            src_ref=sbuf.at[1 - core, q], dst_ref=pbuf.at[q],
            send_sem=p_send.at[q], recv_sem=p_recv.at[q],
            device_id=(mate, ml), device_id_type=MESH)

    def chip_copy(q, source):
        return pltpu.make_async_remote_copy(
            src_ref=sbuf.at[core, q], dst_ref=rbuf.at[source],
            send_sem=r_send.at[q], recv_sem=r_recv.at[source],
            device_id=(q * 2 + core, ml), device_id_type=MESH)

    def finish(q):
        mate_copy(q).wait_recv()
        sbuf[core, q] = sbuf[core, q] + pbuf[q]

    def back(i, carry):
        q = lax.rem(z + 1 + i, nz)

        def back_unit(b, inner_carry):
            unit = q * nb + b
            pair = fpair[...]
            dims = (((1,), (1,)), ((), ()))
            summed = (
                lax.dot_general(kh[unit], pair, dims, preferred_element_type=jnp.float32)
                + lax.dot_general(kl[unit], pair, dims, preferred_element_type=jnp.float32))
            summed = summed + pltpu.roll(summed, targets, 1)
            at = pl.ds(pl.multiple_of(b * half, half), half)
            for c in range(2):
                low = c * LM_BLOCK
                sbuf[c, q, at, :] = jnp.where(
                    lane < targets, summed[low:low + half], summed[low + half:low + LM_BLOCK])
            return inner_carry

        lax.fori_loop(0, nb, back_unit, 0)
        mate_copy(q).start()

        @pl.when(i > 0)
        def _():
            before = lax.rem(z + i, nz)
            finish(before)
            chip_copy(before, z).start()
        return carry

    lax.fori_loop(0, nz, back, 0)
    finish(z)
    result = sbuf[core, z]
    for off in range(1, nz):
        source = lax.rem(z + off, nz)
        chip_copy(source, source).wait_recv()
        result = result + rbuf[source]
    result = result / total_docs
    for b in range(nb):
        piece = result[b * half:(b + 1) * half]
        out_ref[b * LM_BLOCK:b * LM_BLOCK + half, :] = piece[:, :targets]
        out_ref[b * LM_BLOCK + half:(b + 1) * LM_BLOCK, :] = piece[:, targets:]

    def end_own(b, carry):
        for way, there, device in ways:
            @pl.when(there)
            def _():
                own_copy(b, way, device).wait_send()
        own_copy(b, 2, mate).wait_send()
        return carry

    lax.fori_loop(0, nb, end_own, 0)
    for way, there, device in ways:
        @pl.when(there)
        def _():
            own_coef(way, device).wait_send()
    own_coef(2, mate).wait_send()

    def end_rounds(r, carry):
        for way, there, device in ways:
            q, b, valid = place(r, way)
            onward = z + (1 - 2 * way)

            @pl.when(valid)
            def _():
                slot = q * 2 + core
                on = (onward >= 0) & (onward < nz)
                @pl.when(on)
                def _():
                    forward(slot, b, fz_send.at[q, b], onward * 2 + core).wait_send()
                forward(slot, b, fp_send.at[q, b], mate).wait_send()
                @pl.when(b == 0)
                def _():
                    @pl.when(on)
                    def _():
                        forward_coef(slot, cfz_send.at[q], onward * 2 + core).wait_send()
                    forward_coef(slot, cfp_send.at[q], mate).wait_send()
        return carry

    lax.fori_loop(nb, nz * nb, end_rounds, 0)
    for off in range(1, land_count):
        fit_out(off).wait_send()
        full_copy(ml, off, ml).wait_send()
    for off in range(nz):
        mate_copy(lax.rem(z + off, nz)).wait_send()
    for off in range(1, nz):
        chip_copy(lax.rem(z + off, nz), z).wait_send()


def on_device(doc_values, doc_blocks, land_values, land_blocks, coefficients):
    dp_count = lax.axis_size("dp")
    land_count = lax.axis_size("land")
    docs = doc_values.shape[0]
    own = land_values.shape[0]
    targets = coefficients.shape[1]
    width = ACTIVE * TERM_BLOCK
    nz, nb, nd = dp_count // 2, own // LM_BLOCK, docs // DOC_BLOCK
    table = land_blocks.reshape(dp_count, land_count, nb, LAND_ACTIVE)
    table = lax.dynamic_index_in_dim(table, lax.axis_index("land"), axis=1, keepdims=False)
    table = table.reshape(dp_count * nb, LAND_ACTIVE)
    same = doc_blocks[None, :, :, None] == table[:, None, None, :]
    spots = jnp.where(same, jnp.arange(LAND_ACTIVE, dtype=jnp.int32), LAND_ACTIVE)
    pos = jnp.min(spots, axis=3).reshape(-1)
    dma = pltpu.SemaphoreType.DMA
    vmem = pl.BlockSpec(memory_space=pltpu.VMEM)
    units = nz * nb
    pairs = docs * dp_count * own
    half = own // 2
    return pl.pallas_call(
        functools.partial(fused_kernel, dp_count, land_count, float(docs * dp_count)),
        out_shape=jax.ShapeDtypeStruct((own, targets), jnp.float32),
        in_specs=[pl.BlockSpec(memory_space=pltpu.SMEM), vmem, vmem, vmem],
        out_specs=vmem,
        scratch_shapes=[
            pltpu.VMEM((dp_count, nb, LM_BLOCK, width), jnp.bfloat16),
            pltpu.VMEM((dp_count, targets, own), jnp.bfloat16),
            pltpu.VMEM((LAND_ACTIVE + 1, 2 * LM_BLOCK, TERM_BLOCK), jnp.bfloat16),
            pltpu.VMEM((units, 2 * LM_BLOCK, docs), jnp.bfloat16),
            pltpu.VMEM((units, 2 * LM_BLOCK, docs), jnp.bfloat16),
            pltpu.VMEM((nd, 8, DOC_BLOCK), jnp.float32),
            pltpu.VMEM((targets, docs), jnp.float32),
            pltpu.VMEM((land_count, targets // land_count, docs), jnp.float32),
            pltpu.VMEM((targets, docs), jnp.float32),
            pltpu.VMEM((2 * targets, docs), jnp.bfloat16),
            pltpu.VMEM((2, nz, half, 2 * targets), jnp.float32),
            pltpu.VMEM((nz, half, 2 * targets), jnp.float32),
            pltpu.VMEM((nz, half, 2 * targets), jnp.float32),
            dma((2,)), dma((3, nb)), dma((3,)), dma((nz, nb)), dma((nz, nb)), dma((nz,)), dma((nz,)),
            dma((dp_count, nb)), dma((dp_count,)),
            dma((land_count,)), dma((land_count,)), dma((land_count,)), dma((land_count,)),
            dma((nz,)), dma((nz,)), dma((nz,)), dma((nz,)),
        ],
        compiler_params=pltpu.CompilerParams(
            collective_id=0, has_side_effects=True, vmem_limit_bytes=60 * 1024 * 1024),
        cost_estimate=pl.CostEstimate(
            flops=2 * pairs * (width + 6 * targets), bytes_accessed=16 * 1024 * 1024,
            transcendentals=pairs),
    )(
        pos,
        doc_values.reshape(nd, DOC_BLOCK, width),
        land_values.reshape(nb, LM_BLOCK, width),
        coefficients.T,
    )


def solution(mesh):
    placed = (P("dp", None), P("dp", None), P(("dp", "land"), None), P(), P(("dp", "land"), None))
    return jax.shard_map(
        on_device, mesh=mesh, in_specs=placed, out_specs=P(("dp", "land"), None), check_vma=False
    )
```

```python
import functools
import jax
import jax.numpy as jnp
from jax import lax
from jax.experimental import pallas as pl
from jax.experimental.pallas import tpu as pltpu
from jax.sharding import PartitionSpec as P

TERM_BLOCK = 128
ACTIVE = 8
LAND_ACTIVE = 8
DOC_BLOCK = 128
LM_BLOCK = 128
SHARPNESS = 2.0
LOG2E = 1.4426950408889634
EPS = 1e-06
MESH = pl.DeviceIdType.MESH


def row_squares(rows):
    wide = rows.astype(jnp.float32)
    return jnp.sum(wide * wide, axis=1, keepdims=True)


def fused_kernel(
    dp_count, land_count, total_docs,
    pos_ref, doc_ref, land_ref, coef_ref, out_ref,
    lbuf, cbuf, work, kh, kl, dnorm, fit, fpart, full, fpair, sbuf, pbuf, rbuf,
    local_sem, own_send, own_csend, fz_send, fp_send, cfz_send, cfp_send, lrecv, crecv,
    f1_send, f1_recv, f2_send, f2_recv, p_send, p_recv, r_send, r_recv,
):
    nz = dp_count // 2
    nb = land_ref.shape[0]
    nd = doc_ref.shape[0]
    group = 6 if nd % 6 == 0 else 2
    docs = nd * DOC_BLOCK
    targets = coef_ref.shape[0]
    part_rows = targets // land_count
    me = lax.axis_index("dp")
    ml = lax.axis_index("land")
    z = me // 2
    core = me % 2
    mate = z * 2 + (1 - core)

    barrier = pltpu.get_barrier_semaphore()
    pl.semaphore_signal(barrier, inc=1, device_id=(mate, ml), device_id_type=MESH)
    for off in range(1, nz):
        other = lax.rem(z + off, nz) * 2 + core
        pl.semaphore_signal(barrier, inc=1, device_id=(other, ml), device_id_type=MESH)
    for off in range(1, land_count):
        other = lax.rem(ml + off, land_count)
        pl.semaphore_signal(barrier, inc=1, device_id=(me, other), device_id_type=MESH)
    pl.semaphore_wait(barrier, 1 + (nz - 1) + (land_count - 1))

    def own_copy(b, way, device):
        return pltpu.make_async_remote_copy(
            src_ref=land_ref.at[b], dst_ref=lbuf.at[me, b],
            send_sem=own_send.at[way, b], recv_sem=lrecv.at[me, b],
            device_id=(device, ml), device_id_type=MESH)

    def own_coef(way, device):
        return pltpu.make_async_remote_copy(
            src_ref=coef_ref, dst_ref=cbuf.at[me],
            send_sem=own_csend.at[way], recv_sem=crecv.at[me],
            device_id=(device, ml), device_id_type=MESH)

    def forward(slot, b, send, device):
        return pltpu.make_async_remote_copy(
            src_ref=lbuf.at[slot, b], dst_ref=lbuf.at[slot, b],
            send_sem=send, recv_sem=lrecv.at[slot, b],
            device_id=(device, ml), device_id_type=MESH)

    def forward_coef(slot, send, device):
        return pltpu.make_async_remote_copy(
            src_ref=cbuf.at[slot], dst_ref=cbuf.at[slot],
            send_sem=send, recv_sem=crecv.at[slot],
            device_id=(device, ml), device_id_type=MESH)

    ways = ((0, z > 0, me - 2), (1, z < nz - 1, me + 2))

    def start_own(b, carry):
        for way, there, device in ways:
            @pl.when(there)
            def _():
                @pl.when(b == 0)
                def _():
                    own_coef(way, device).start()
                own_copy(b, way, device).start()

        @pl.when(b == 0)
        def _():
            own_coef(2, mate).start()
        own_copy(b, 2, mate).start()
        return carry

    lax.fori_loop(0, nb, start_own, 0)
    keep_land = pltpu.make_async_copy(land_ref, lbuf.at[me], local_sem.at[0])
    keep_coef = pltpu.make_async_copy(coef_ref, cbuf.at[me], local_sem.at[1])
    keep_land.start()
    keep_coef.start()

    work[LAND_ACTIVE] = jnp.zeros((2 * LM_BLOCK, TERM_BLOCK), jnp.bfloat16)
    fit[...] = jnp.zeros_like(fit)

    def doc_norms(d, carry):
        scale = (2.0 * SHARPNESS * LOG2E) * lax.rsqrt(row_squares(doc_ref[d]) + EPS)
        dnorm[d] = jnp.transpose(jnp.broadcast_to(scale, (DOC_BLOCK, DOC_BLOCK)))[0:8, :]
        return carry

    lax.fori_loop(0, nd, doc_norms, 0)
    keep_land.wait()
    keep_coef.wait()

    def compute(q, b):
        norms = []
        for c in range(2):
            for a in range(LAND_ACTIVE):
                work[a, c * LM_BLOCK:(c + 1) * LM_BLOCK, :] = (
                    lbuf[q * 2 + c, b, :, a * TERM_BLOCK:(a + 1) * TERM_BLOCK])
            norms.append(lax.rsqrt(row_squares(lbuf[q * 2 + c, b]) + EPS))
        norm = jnp.concatenate(norms, axis=0)
        start = pl.multiple_of(b * LM_BLOCK, LM_BLOCK)
        coef = jnp.concatenate(
            [cbuf[q * 2, :, pl.ds(start, LM_BLOCK)], cbuf[q * 2 + 1, :, pl.ds(start, LM_BLOCK)]],
            axis=1)
        unit = q * nb + b

        def doc_pair(d0):
            highs, lows = [], []
            for h in range(2):
                d = d0 + h
                sides = []
                for c in range(2):
                    first = (((q * 2 + c) * nb + b) * nd + d) * ACTIVE
                    sides.append(jnp.concatenate(
                        [work[pos_ref[first + a], c * LM_BLOCK:(c + 1) * LM_BLOCK, :]
                         for a in range(ACTIVE)], axis=1))
                aligned = jnp.concatenate(sides, axis=0)
                inner = lax.dot_general(
                    aligned, doc_ref[d], (((1,), (1,)), ((), ())),
                    preferred_element_type=jnp.float32)
                power = inner * norm * dnorm[d][0:1, :] - (2.0 * SHARPNESS * LOG2E)
                kernel = jnp.exp2(power)
                high = kernel.astype(jnp.bfloat16)
                highs.append(high)
                lows.append((kernel - high.astype(jnp.float32)).astype(jnp.bfloat16))
            high = jnp.concatenate(highs, axis=1)
            low = jnp.concatenate(lows, axis=1)
            cols = pl.ds(pl.multiple_of(d0 * DOC_BLOCK, 2 * DOC_BLOCK), 2 * DOC_BLOCK)
            kh[unit, :, cols] = high
            kl[unit, :, cols] = low
            fit[:, cols] += (
                jnp.dot(coef, high, preferred_element_type=jnp.float32)
                + jnp.dot(coef, low, preferred_element_type=jnp.float32))

        def doc_group(i, carry):
            for pair in range(group // 2):
                doc_pair(i * group + 2 * pair)
            return carry

        lax.fori_loop(0, nd // group, doc_group, 0)

    def place(r, way):
        hops = r // nb
        q = z + hops * (2 * way - 1)
        return q, r % nb, (q >= 0) & (q < nz)

    def rounds(r, carry):
        for way, there, device in ways:
            @pl.when(r >= nb)
            def _():
                q, b, valid = place(r, way)
                onward = z + (1 - 2 * way)

                @pl.when(valid)
                def _():
                    slot = q * 2 + core
                    forward(slot, b, fp_send.at[q, b], mate).wait_recv()
                    @pl.when((onward >= 0) & (onward < nz))
                    def _():
                        forward(slot, b, fz_send.at[q, b], onward * 2 + core).start()
                    forward(slot, b, fp_send.at[q, b], mate).start()
                    @pl.when(b == 0)
                    def _():
                        forward_coef(slot, cfp_send.at[q], mate).wait_recv()
                        @pl.when((onward >= 0) & (onward < nz))
                        def _():
                            forward_coef(slot, cfz_send.at[q], onward * 2 + core).start()
                        forward_coef(slot, cfp_send.at[q], mate).start()

        def one_way(way, inner_carry):
            q, b, valid = place(r, way)

            @pl.when(valid & ((r >= nb) | (way == 0)))
            def _():
                slot = q * 2 + 1 - core
                forward(slot, b, fp_send.at[q, b], mate).wait_recv()
                @pl.when(b == 0)
                def _():
                    forward_coef(slot, cfp_send.at[q], mate).wait_recv()
                compute(q, b)
            return inner_carry

        lax.fori_loop(0, 2, one_way, 0)
        return carry

    lax.fori_loop(0, nz * nb, rounds, 0)

    def fit_out(off):
        peer = lax.rem(ml + off, land_count)
        rows = pl.ds(pl.multiple_of(peer * part_rows, part_rows), part_rows)
        return pltpu.make_async_remote_copy(
            src_ref=fit.at[rows], dst_ref=fpart.at[ml],
            send_sem=f1_send.at[off], recv_sem=f1_recv.at[ml],
            device_id=(me, peer), device_id_type=MESH)

    def fit_in(off):
        peer = lax.rem(ml + off, land_count)
        rows = pl.ds(pl.multiple_of(ml * part_rows, part_rows), part_rows)
        return pltpu.make_async_remote_copy(
            src_ref=fit.at[rows], dst_ref=fpart.at[peer],
            send_sem=f1_send.at[off], recv_sem=f1_recv.at[peer],
            device_id=(me, peer), device_id_type=MESH)

    def full_copy(owner, off, sem_slot):
        peer = lax.rem(ml + off, land_count)
        rows = pl.ds(pl.multiple_of(owner * part_rows, part_rows), part_rows)
        return pltpu.make_async_remote_copy(
            src_ref=full.at[rows], dst_ref=full.at[rows],
            send_sem=f2_send.at[off], recv_sem=f2_recv.at[sem_slot],
            device_id=(me, peer), device_id_type=MESH)

    for off in range(1, land_count):
        fit_out(off).start()
    mine = pl.ds(pl.multiple_of(ml * part_rows, part_rows), part_rows)
    total = fit[mine, :]
    for off in range(1, land_count):
        fit_in(off).wait_recv()
        total = total + fpart[lax.rem(ml + off, land_count)]
    full[mine, :] = total
    for off in range(1, land_count):
        full_copy(ml, off, ml).start()
    for off in range(1, land_count):
        peer = lax.rem(ml + off, land_count)
        full_copy(peer, off, peer).wait_recv()
    fitted = full[...]
    fitted_high = fitted.astype(jnp.bfloat16)
    fpair[0:targets, :] = fitted_high
    fpair[targets:, :] = (fitted - fitted_high.astype(jnp.float32)).astype(jnp.bfloat16)

    half = LM_BLOCK // 2
    lane = lax.broadcasted_iota(jnp.int32, (half, 2 * targets), 1)

    def mate_copy(q):
        return pltpu.make_async_remote_copy(
            src_ref=sbuf.at[1 - core, q], dst_ref=pbuf.at[q],
            send_sem=p_send.at[q], recv_sem=p_recv.at[q],
            device_id=(mate, ml), device_id_type=MESH)

    def chip_copy(q, source):
        return pltpu.make_async_remote_copy(
            src_ref=sbuf.at[core, q], dst_ref=rbuf.at[source],
            send_sem=r_send.at[q], recv_sem=r_recv.at[source],
            device_id=(q * 2 + core, ml), device_id_type=MESH)

    def finish(q):
        mate_copy(q).wait_recv()
        sbuf[core, q] = sbuf[core, q] + pbuf[q]

    def back(i, carry):
        q = lax.rem(z + 1 + i, nz)

        pair = fpair[...]
        for b in range(nb):
            unit = q * nb + b
            both = lax.dot_general(
                jnp.concatenate([kh[unit], kl[unit]], axis=0), pair, (((1,), (1,)), ((), ())),
                preferred_element_type=jnp.float32)
            summed = both[:2 * LM_BLOCK] + both[2 * LM_BLOCK:]
            summed = summed + pltpu.roll(summed, targets, 1)
            for c in range(2):
                low = c * LM_BLOCK
                sbuf[c, q, b * half:(b + 1) * half, :] = jnp.where(
                    lane < targets, summed[low:low + half], summed[low + half:low + LM_BLOCK])
        mate_copy(q).start()

        @pl.when(i > 0)
        def _():
            before = lax.rem(z + i, nz)
            finish(before)
            chip_copy(before, z).start()
        return carry

    lax.fori_loop(0, nz, back, 0)
    finish(z)
    result = sbuf[core, z]
    for off in range(1, nz):
        source = lax.rem(z + off, nz)
        chip_copy(source, source).wait_recv()
        result = result + rbuf[source]
    result = result / total_docs
    for b in range(nb):
        piece = result[b * half:(b + 1) * half]
        out_ref[b * LM_BLOCK:b * LM_BLOCK + half, :] = piece[:, :targets]
        out_ref[b * LM_BLOCK + half:(b + 1) * LM_BLOCK, :] = piece[:, targets:]

    def end_own(b, carry):
        for way, there, device in ways:
            @pl.when(there)
            def _():
                own_copy(b, way, device).wait_send()
        own_copy(b, 2, mate).wait_send()
        return carry

    lax.fori_loop(0, nb, end_own, 0)
    for way, there, device in ways:
        @pl.when(there)
        def _():
            own_coef(way, device).wait_send()
    own_coef(2, mate).wait_send()

    def end_rounds(r, carry):
        for way, there, device in ways:
            q, b, valid = place(r, way)
            onward = z + (1 - 2 * way)

            @pl.when(valid)
            def _():
                slot = q * 2 + core
                on = (onward >= 0) & (onward < nz)
                @pl.when(on)
                def _():
                    forward(slot, b, fz_send.at[q, b], onward * 2 + core).wait_send()
                forward(slot, b, fp_send.at[q, b], mate).wait_send()
                @pl.when(b == 0)
                def _():
                    @pl.when(on)
                    def _():
                        forward_coef(slot, cfz_send.at[q], onward * 2 + core).wait_send()
                    forward_coef(slot, cfp_send.at[q], mate).wait_send()
        return carry

    lax.fori_loop(nb, nz * nb, end_rounds, 0)
    for off in range(1, land_count):
        fit_out(off).wait_send()
        full_copy(ml, off, ml).wait_send()
    for off in range(nz):
        mate_copy(lax.rem(z + off, nz)).wait_send()
    for off in range(1, nz):
        chip_copy(lax.rem(z + off, nz), z).wait_send()


def on_device(doc_values, doc_blocks, land_values, land_blocks, coefficients):
    dp_count = lax.axis_size("dp")
    land_count = lax.axis_size("land")
    docs = doc_values.shape[0]
    own = land_values.shape[0]
    targets = coefficients.shape[1]
    width = ACTIVE * TERM_BLOCK
    nz, nb, nd = dp_count // 2, own // LM_BLOCK, docs // DOC_BLOCK
    table = land_blocks.reshape(dp_count, land_count, nb, LAND_ACTIVE)
    table = lax.dynamic_index_in_dim(table, lax.axis_index("land"), axis=1, keepdims=False)
    table = table.reshape(dp_count * nb, LAND_ACTIVE)
    same = doc_blocks[None, :, :, None] == table[:, None, None, :]
    spots = jnp.where(same, jnp.arange(LAND_ACTIVE, dtype=jnp.int32), LAND_ACTIVE)
    pos = jnp.min(spots, axis=3).reshape(-1)
    dma = pltpu.SemaphoreType.DMA
    vmem = pl.BlockSpec(memory_space=pltpu.VMEM)
    units = nz * nb
    pairs = docs * dp_count * own
    half = own // 2
    return pl.pallas_call(
        functools.partial(fused_kernel, dp_count, land_count, float(docs * dp_count)),
        out_shape=jax.ShapeDtypeStruct((own, targets), jnp.float32),
        in_specs=[pl.BlockSpec(memory_space=pltpu.SMEM), vmem, vmem, vmem],
        out_specs=vmem,
        scratch_shapes=[
            pltpu.VMEM((dp_count, nb, LM_BLOCK, width), jnp.bfloat16),
            pltpu.VMEM((dp_count, targets, own), jnp.bfloat16),
            pltpu.VMEM((LAND_ACTIVE + 1, 2 * LM_BLOCK, TERM_BLOCK), jnp.bfloat16),
            pltpu.VMEM((units, 2 * LM_BLOCK, docs), jnp.bfloat16),
            pltpu.VMEM((units, 2 * LM_BLOCK, docs), jnp.bfloat16),
            pltpu.VMEM((nd, 8, DOC_BLOCK), jnp.float32),
            pltpu.VMEM((targets, docs), jnp.float32),
            pltpu.VMEM((land_count, targets // land_count, docs), jnp.float32),
            pltpu.VMEM((targets, docs), jnp.float32),
            pltpu.VMEM((2 * targets, docs), jnp.bfloat16),
            pltpu.VMEM((2, nz, half, 2 * targets), jnp.float32),
            pltpu.VMEM((nz, half, 2 * targets), jnp.float32),
            pltpu.VMEM((nz, half, 2 * targets), jnp.float32),
            dma((2,)), dma((3, nb)), dma((3,)), dma((nz, nb)), dma((nz, nb)), dma((nz,)), dma((nz,)),
            dma((dp_count, nb)), dma((dp_count,)),
            dma((land_count,)), dma((land_count,)), dma((land_count,)), dma((land_count,)),
            dma((nz,)), dma((nz,)), dma((nz,)), dma((nz,)),
        ],
        compiler_params=pltpu.CompilerParams(
            collective_id=0, has_side_effects=True, vmem_limit_bytes=60 * 1024 * 1024),
        cost_estimate=pl.CostEstimate(
            flops=2 * pairs * (width + 6 * targets), bytes_accessed=16 * 1024 * 1024,
            transcendentals=pairs),
    )(
        pos,
        doc_values.reshape(nd, DOC_BLOCK, width),
        land_values.reshape(nb, LM_BLOCK, width),
        coefficients.T,
    )


def solution(mesh):
    placed = (P("dp", None), P("dp", None), P(("dp", "land"), None), P(), P(("dp", "land"), None))
    return jax.shard_map(
        on_device, mesh=mesh, in_specs=placed, out_specs=P(("dp", "land"), None), check_vma=False
    )
```

```python
import functools
import jax
import jax.numpy as jnp
from jax import lax
from jax.experimental import pallas as pl
from jax.experimental.pallas import tpu as pltpu
from jax.sharding import PartitionSpec as P

TERM_BLOCK = 128
ACTIVE = 8
LAND_ACTIVE = 8
DOC_BLOCK = 128
LM_BLOCK = 128
SHARPNESS = 2.0
LOG2E = 1.4426950408889634
EPS = 1e-06
MESH = pl.DeviceIdType.MESH


def row_squares(rows):
    wide = rows.astype(jnp.float32)
    return jnp.sum(wide * wide, axis=1, keepdims=True)


def fused_kernel(
    dp_count, land_count, total_docs,
    pos_ref, doc_ref, land_ref, coef_ref, out_ref,
    lbuf, cbuf, work, kh, kl, dnorm, fit, fpart, full, fpair, sbuf, pbuf, rbuf,
    local_sem, own_send, own_csend, fz_send, fp_send, cfz_send, cfp_send, lrecv, crecv,
    f1_send, f1_recv, f2_send, f2_recv, p_send, p_recv, r_send, r_recv,
):
    nz = dp_count // 2
    nb = land_ref.shape[0]
    nd = doc_ref.shape[0]
    group = 12 if nd % 12 == 0 else 2
    docs = nd * DOC_BLOCK
    targets = coef_ref.shape[0]
    part_rows = targets // land_count
    me = lax.axis_index("dp")
    ml = lax.axis_index("land")
    z = me // 2
    core = me % 2
    mate = z * 2 + (1 - core)

    barrier = pltpu.get_barrier_semaphore()
    pl.semaphore_signal(barrier, inc=1, device_id=(mate, ml), device_id_type=MESH)
    for off in range(1, nz):
        other = lax.rem(z + off, nz) * 2 + core
        pl.semaphore_signal(barrier, inc=1, device_id=(other, ml), device_id_type=MESH)
    for off in range(1, land_count):
        other = lax.rem(ml + off, land_count)
        pl.semaphore_signal(barrier, inc=1, device_id=(me, other), device_id_type=MESH)
    pl.semaphore_wait(barrier, 1 + (nz - 1) + (land_count - 1))

    def own_copy(b, way, device):
        return pltpu.make_async_remote_copy(
            src_ref=land_ref.at[b], dst_ref=lbuf.at[me, b],
            send_sem=own_send.at[way, b], recv_sem=lrecv.at[me, b],
            device_id=(device, ml), device_id_type=MESH)

    def own_coef(way, device):
        return pltpu.make_async_remote_copy(
            src_ref=coef_ref, dst_ref=cbuf.at[me],
            send_sem=own_csend.at[way], recv_sem=crecv.at[me],
            device_id=(device, ml), device_id_type=MESH)

    def forward(slot, b, send, device):
        return pltpu.make_async_remote_copy(
            src_ref=lbuf.at[slot, b], dst_ref=lbuf.at[slot, b],
            send_sem=send, recv_sem=lrecv.at[slot, b],
            device_id=(device, ml), device_id_type=MESH)

    def forward_coef(slot, send, device):
        return pltpu.make_async_remote_copy(
            src_ref=cbuf.at[slot], dst_ref=cbuf.at[slot],
            send_sem=send, recv_sem=crecv.at[slot],
            device_id=(device, ml), device_id_type=MESH)

    ways = ((0, z > 0, me - 2), (1, z < nz - 1, me + 2))

    def start_own(b, carry):
        for way, there, device in ways:
            @pl.when(there)
            def _():
                @pl.when(b == 0)
                def _():
                    own_coef(way, device).start()
                own_copy(b, way, device).start()

        @pl.when(b == 0)
        def _():
            own_coef(2, mate).start()
        own_copy(b, 2, mate).start()
        return carry

    lax.fori_loop(0, nb, start_own, 0)
    keep_land = pltpu.make_async_copy(land_ref, lbuf.at[me], local_sem.at[0])
    keep_coef = pltpu.make_async_copy(coef_ref, cbuf.at[me], local_sem.at[1])
    keep_land.start()
    keep_coef.start()

    work[LAND_ACTIVE] = jnp.zeros((2 * LM_BLOCK, TERM_BLOCK), jnp.bfloat16)
    fit[...] = jnp.zeros_like(fit)

    def doc_norms(d, carry):
        scale = (2.0 * SHARPNESS * LOG2E) * lax.rsqrt(row_squares(doc_ref[d]) + EPS)
        dnorm[d] = jnp.transpose(jnp.broadcast_to(scale, (DOC_BLOCK, DOC_BLOCK)))[0:8, :]
        return carry

    lax.fori_loop(0, nd, doc_norms, 0)
    keep_land.wait()
    keep_coef.wait()

    def compute(q, b):
        norms = []
        for c in range(2):
            for a in range(LAND_ACTIVE):
                work[a, c * LM_BLOCK:(c + 1) * LM_BLOCK, :] = (
                    lbuf[q * 2 + c, b, :, a * TERM_BLOCK:(a + 1) * TERM_BLOCK])
            norms.append(lax.rsqrt(row_squares(lbuf[q * 2 + c, b]) + EPS))
        norm = jnp.concatenate(norms, axis=0)
        start = pl.multiple_of(b * LM_BLOCK, LM_BLOCK)
        coef = jnp.concatenate(
            [cbuf[q * 2, :, pl.ds(start, LM_BLOCK)], cbuf[q * 2 + 1, :, pl.ds(start, LM_BLOCK)]],
            axis=1)
        unit = q * nb + b

        def doc_pair(d0):
            highs, lows = [], []
            for h in range(2):
                d = d0 + h
                sides = []
                for c in range(2):
                    first = (((q * 2 + c) * nb + b) * nd + d) * ACTIVE
                    sides.append(jnp.concatenate(
                        [work[pos_ref[first + a], c * LM_BLOCK:(c + 1) * LM_BLOCK, :]
                         for a in range(ACTIVE)], axis=1))
                aligned = jnp.concatenate(sides, axis=0)
                inner = lax.dot_general(
                    aligned, doc_ref[d], (((1,), (1,)), ((), ())),
                    preferred_element_type=jnp.float32)
                power = inner * norm * dnorm[d][0:1, :] - (2.0 * SHARPNESS * LOG2E)
                kernel = jnp.exp2(power)
                high = kernel.astype(jnp.bfloat16)
                highs.append(high)
                lows.append((kernel - high.astype(jnp.float32)).astype(jnp.bfloat16))
            high = jnp.concatenate(highs, axis=1)
            low = jnp.concatenate(lows, axis=1)
            cols = pl.ds(pl.multiple_of(d0 * DOC_BLOCK, 2 * DOC_BLOCK), 2 * DOC_BLOCK)
            kh[unit, :, cols] = high
            kl[unit, :, cols] = low
            fit[:, cols] += (
                jnp.dot(coef, high, preferred_element_type=jnp.float32)
                + jnp.dot(coef, low, preferred_element_type=jnp.float32))

        def doc_group(i, carry):
            for pair in range(group // 2):
                doc_pair(i * group + 2 * pair)
            return carry

        lax.fori_loop(0, nd // group, doc_group, 0)

    def place(r, way):
        hops = r // nb
        q = z + hops * (2 * way - 1)
        return q, r % nb, (q >= 0) & (q < nz)

    def rounds(r, carry):
        for way, there, device in ways:
            @pl.when(r >= nb)
            def _():
                q, b, valid = place(r, way)
                onward = z + (1 - 2 * way)

                @pl.when(valid)
                def _():
                    slot = q * 2 + core
                    forward(slot, b, fp_send.at[q, b], mate).wait_recv()
                    @pl.when((onward >= 0) & (onward < nz))
                    def _():
                        forward(slot, b, fz_send.at[q, b], onward * 2 + core).start()
                    forward(slot, b, fp_send.at[q, b], mate).start()
                    @pl.when(b == 0)
                    def _():
                        forward_coef(slot, cfp_send.at[q], mate).wait_recv()
                        @pl.when((onward >= 0) & (onward < nz))
                        def _():
                            forward_coef(slot, cfz_send.at[q], onward * 2 + core).start()
                        forward_coef(slot, cfp_send.at[q], mate).start()

        def one_way(way, inner_carry):
            q, b, valid = place(r, way)

            @pl.when(valid & ((r >= nb) | (way == 0)))
            def _():
                slot = q * 2 + 1 - core
                forward(slot, b, fp_send.at[q, b], mate).wait_recv()
                @pl.when(b == 0)
                def _():
                    forward_coef(slot, cfp_send.at[q], mate).wait_recv()
                compute(q, b)
            return inner_carry

        lax.fori_loop(0, 2, one_way, 0)
        return carry

    lax.fori_loop(0, nz * nb, rounds, 0)

    def fit_out(off):
        peer = lax.rem(ml + off, land_count)
        rows = pl.ds(pl.multiple_of(peer * part_rows, part_rows), part_rows)
        return pltpu.make_async_remote_copy(
            src_ref=fit.at[rows], dst_ref=fpart.at[ml],
            send_sem=f1_send.at[off], recv_sem=f1_recv.at[ml],
            device_id=(me, peer), device_id_type=MESH)

    def fit_in(off):
        peer = lax.rem(ml + off, land_count)
        rows = pl.ds(pl.multiple_of(ml * part_rows, part_rows), part_rows)
        return pltpu.make_async_remote_copy(
            src_ref=fit.at[rows], dst_ref=fpart.at[peer],
            send_sem=f1_send.at[off], recv_sem=f1_recv.at[peer],
            device_id=(me, peer), device_id_type=MESH)

    def full_copy(owner, off, sem_slot):
        peer = lax.rem(ml + off, land_count)
        rows = pl.ds(pl.multiple_of(owner * part_rows, part_rows), part_rows)
        return pltpu.make_async_remote_copy(
            src_ref=full.at[rows], dst_ref=full.at[rows],
            send_sem=f2_send.at[off], recv_sem=f2_recv.at[sem_slot],
            device_id=(me, peer), device_id_type=MESH)

    for off in range(1, land_count):
        fit_out(off).start()
    mine = pl.ds(pl.multiple_of(ml * part_rows, part_rows), part_rows)
    total = fit[mine, :]
    for off in range(1, land_count):
        fit_in(off).wait_recv()
        total = total + fpart[lax.rem(ml + off, land_count)]
    full[mine, :] = total
    for off in range(1, land_count):
        full_copy(ml, off, ml).start()
    for off in range(1, land_count):
        peer = lax.rem(ml + off, land_count)
        full_copy(peer, off, peer).wait_recv()
    fitted = full[...]
    fitted_high = fitted.astype(jnp.bfloat16)
    fpair[0:targets, :] = fitted_high
    fpair[targets:, :] = (fitted - fitted_high.astype(jnp.float32)).astype(jnp.bfloat16)

    half = LM_BLOCK // 2
    lane = lax.broadcasted_iota(jnp.int32, (half, 2 * targets), 1)

    def mate_copy(q):
        return pltpu.make_async_remote_copy(
            src_ref=sbuf.at[1 - core, q], dst_ref=pbuf.at[q],
            send_sem=p_send.at[q], recv_sem=p_recv.at[q],
            device_id=(mate, ml), device_id_type=MESH)

    def chip_copy(q, source):
        return pltpu.make_async_remote_copy(
            src_ref=sbuf.at[core, q], dst_ref=rbuf.at[source],
            send_sem=r_send.at[q], recv_sem=r_recv.at[source],
            device_id=(q * 2 + core, ml), device_id_type=MESH)

    def finish(q):
        mate_copy(q).wait_recv()
        sbuf[core, q] = sbuf[core, q] + pbuf[q]

    def back(i, carry):
        q = lax.rem(z + 1 + i, nz)

        pair = fpair[...]
        for b in range(nb):
            unit = q * nb + b
            both = lax.dot_general(
                jnp.concatenate([kh[unit], kl[unit]], axis=0), pair, (((1,), (1,)), ((), ())),
                preferred_element_type=jnp.float32)
            summed = both[:2 * LM_BLOCK] + both[2 * LM_BLOCK:]
            summed = summed + pltpu.roll(summed, targets, 1)
            for c in range(2):
                low = c * LM_BLOCK
                sbuf[c, q, b * half:(b + 1) * half, :] = jnp.where(
                    lane < targets, summed[low:low + half], summed[low + half:low + LM_BLOCK])
            if b == min(1, nb - 1):
                @pl.when(i > 0)
                def _():
                    before = lax.rem(z + i, nz)
                    finish(before)
                    chip_copy(before, z).start()
        mate_copy(q).start()
        return carry

    lax.fori_loop(0, nz, back, 0)
    finish(z)
    result = sbuf[core, z]
    for off in range(1, nz):
        source = lax.rem(z + off, nz)
        chip_copy(source, source).wait_recv()
        result = result + rbuf[source]
    result = result / total_docs
    for b in range(nb):
        piece = result[b * half:(b + 1) * half]
        out_ref[b * LM_BLOCK:b * LM_BLOCK + half, :] = piece[:, :targets]
        out_ref[b * LM_BLOCK + half:(b + 1) * LM_BLOCK, :] = piece[:, targets:]

    def end_own(b, carry):
        for way, there, device in ways:
            @pl.when(there)
            def _():
                own_copy(b, way, device).wait_send()
        own_copy(b, 2, mate).wait_send()
        return carry

    lax.fori_loop(0, nb, end_own, 0)
    for way, there, device in ways:
        @pl.when(there)
        def _():
            own_coef(way, device).wait_send()
    own_coef(2, mate).wait_send()

    def end_rounds(r, carry):
        for way, there, device in ways:
            q, b, valid = place(r, way)
            onward = z + (1 - 2 * way)

            @pl.when(valid)
            def _():
                slot = q * 2 + core
                on = (onward >= 0) & (onward < nz)
                @pl.when(on)
                def _():
                    forward(slot, b, fz_send.at[q, b], onward * 2 + core).wait_send()
                forward(slot, b, fp_send.at[q, b], mate).wait_send()
                @pl.when(b == 0)
                def _():
                    @pl.when(on)
                    def _():
                        forward_coef(slot, cfz_send.at[q], onward * 2 + core).wait_send()
                    forward_coef(slot, cfp_send.at[q], mate).wait_send()
        return carry

    lax.fori_loop(nb, nz * nb, end_rounds, 0)
    for off in range(1, land_count):
        fit_out(off).wait_send()
        full_copy(ml, off, ml).wait_send()
    for off in range(nz):
        mate_copy(lax.rem(z + off, nz)).wait_send()
    for off in range(1, nz):
        chip_copy(lax.rem(z + off, nz), z).wait_send()


def on_device(doc_values, doc_blocks, land_values, land_blocks, coefficients):
    dp_count = lax.axis_size("dp")
    land_count = lax.axis_size("land")
    docs = doc_values.shape[0]
    own = land_values.shape[0]
    targets = coefficients.shape[1]
    width = ACTIVE * TERM_BLOCK
    nz, nb, nd = dp_count // 2, own // LM_BLOCK, docs // DOC_BLOCK
    table = land_blocks.reshape(dp_count, land_count, nb, LAND_ACTIVE)
    table = lax.dynamic_index_in_dim(table, lax.axis_index("land"), axis=1, keepdims=False)
    table = table.reshape(dp_count * nb, LAND_ACTIVE)
    same = doc_blocks[None, :, :, None] == table[:, None, None, :]
    spots = jnp.where(same, jnp.arange(LAND_ACTIVE, dtype=jnp.int32), LAND_ACTIVE)
    pos = jnp.min(spots, axis=3).reshape(-1)
    dma = pltpu.SemaphoreType.DMA
    vmem = pl.BlockSpec(memory_space=pltpu.VMEM)
    units = nz * nb
    pairs = docs * dp_count * own
    half = own // 2
    return pl.pallas_call(
        functools.partial(fused_kernel, dp_count, land_count, float(docs * dp_count)),
        out_shape=jax.ShapeDtypeStruct((own, targets), jnp.float32),
        in_specs=[pl.BlockSpec(memory_space=pltpu.SMEM), vmem, vmem, vmem],
        out_specs=vmem,
        scratch_shapes=[
            pltpu.VMEM((dp_count, nb, LM_BLOCK, width), jnp.bfloat16),
            pltpu.VMEM((dp_count, targets, own), jnp.bfloat16),
            pltpu.VMEM((LAND_ACTIVE + 1, 2 * LM_BLOCK, TERM_BLOCK), jnp.bfloat16),
            pltpu.VMEM((units, 2 * LM_BLOCK, docs), jnp.bfloat16),
            pltpu.VMEM((units, 2 * LM_BLOCK, docs), jnp.bfloat16),
            pltpu.VMEM((nd, 8, DOC_BLOCK), jnp.float32),
            pltpu.VMEM((targets, docs), jnp.float32),
            pltpu.VMEM((land_count, targets // land_count, docs), jnp.float32),
            pltpu.VMEM((targets, docs), jnp.float32),
            pltpu.VMEM((2 * targets, docs), jnp.bfloat16),
            pltpu.VMEM((2, nz, half, 2 * targets), jnp.float32),
            pltpu.VMEM((nz, half, 2 * targets), jnp.float32),
            pltpu.VMEM((nz, half, 2 * targets), jnp.float32),
            dma((2,)), dma((3, nb)), dma((3,)), dma((nz, nb)), dma((nz, nb)), dma((nz,)), dma((nz,)),
            dma((dp_count, nb)), dma((dp_count,)),
            dma((land_count,)), dma((land_count,)), dma((land_count,)), dma((land_count,)),
            dma((nz,)), dma((nz,)), dma((nz,)), dma((nz,)),
        ],
        compiler_params=pltpu.CompilerParams(
            collective_id=0, has_side_effects=True, vmem_limit_bytes=60 * 1024 * 1024),
        cost_estimate=pl.CostEstimate(
            flops=2 * pairs * (width + 6 * targets), bytes_accessed=16 * 1024 * 1024,
            transcendentals=pairs),
    )(
        pos,
        doc_values.reshape(nd, DOC_BLOCK, width),
        land_values.reshape(nb, LM_BLOCK, width),
        coefficients.T,
    )


def solution(mesh):
    placed = (P("dp", None), P("dp", None), P(("dp", "land"), None), P(), P(("dp", "land"), None))
    return jax.shard_map(
        on_device, mesh=mesh, in_specs=placed, out_specs=P(("dp", "land"), None), check_vma=False
    )
```
